32 devices in a mesh: gx: 2 (over x), gy: 4 (over y, core), gz: 4 (over z).
Axes of the slice: x: 2, y: 2, z: 4, core: 2. Of those that a mesh axis runs over, the one named last changes fastest.
Arguments:
- node_feats: bfloat16 [64, 16384], P(None, ('gx', 'gy', 'gz')), may hold values from -6 to 6
- edge_vectors: float32 [3, 65536], P(None, ('gx', 'gy', 'gz')), may hold values from -4.95 to 4.95, as said below
- edge_source: int32 [65536], P(('gx', 'gy', 'gz')), may hold values from 0 to 1279
- edge_target: int32 [65536], P(('gx', 'gy', 'gz')), may hold values from 0 to 511
- edge_count: int32 [32], P(('gx', 'gy', 'gz')), may hold values from 1 to 2048, 40960 in all
- halo_index: int32 [6, 4096], P(None, ('gx', 'gy', 'gz')), may hold values from 0 to 511
- atom_species: int32 [16384], P(('gx', 'gy', 'gz')), may hold values from 0 to 3
- site_cotangent: float32 [16384], P(('gx', 'gy', 'gz')), may hold values from -6 to 6
- radial_input: float32 [8, 64], replicated, may hold values from -12 to 12
- radial_hidden: float32 [2, 64, 64], replicated, may hold values from -1.2 to 1.2
- radial_output: float32 [64, 256], replicated, may hold values from -0.75 to 0.75
- degree_mix: float32 [4, 64, 64], replicated, may hold values from -0.75 to 0.75
- species_mix: float32 [4, 64, 64], replicated, may hold values from -0.75 to 0.75
- readout_weights: float32 [2, 64], replicated, may hold values from -0.75 to 0.75
- moment_radial_input: float32 [8, 64], replicated, may hold values from -6 to 6
- moment_radial_hidden: float32 [2, 64, 64], replicated, may hold values from -6 to 6
- moment_radial_output: float32 [64, 256], replicated, may hold values from -6 to 6
- moment_degree_mix: float32 [4, 64, 64], replicated, may hold values from -6 to 6
- moment_species_mix: float32 [4, 64, 64], replicated, may hold values from -6 to 6
- moment_readout_weights: float32 [2, 64], replicated, may hold values from -40 to 40
- square_radial_input: float32 [8, 64], replicated, may hold values from 0.16384 to 0.65536
- square_radial_hidden: float32 [2, 64, 64], replicated, may hold values from 0.16384 to 0.65536
- square_radial_output: float32 [64, 256], replicated, may hold values from 0.16384 to 0.65536
- square_degree_mix: float32 [4, 64, 64], replicated, may hold values from 0.16384 to 0.65536
- square_species_mix: float32 [4, 64, 64], replicated, may hold values from 0.16384 to 0.65536
- square_readout_weights: float32 [2, 64], replicated, may hold values from 4.096 to 16.384
Outputs:
- site_energy: float32 [16384], P(('gx', 'gy', 'gz'))
- feature_grad: float32 [64, 16384], P(None, ('gx', 'gy', 'gz'))
- position_grad: float32 [3, 16384], P(None, ('gx', 'gy', 'gz'))
- updated_radial_input: float32 [8, 64], replicated
- updated_radial_hidden: float32 [2, 64, 64], replicated
- updated_radial_output: float32 [64, 256], replicated
- updated_degree_mix: float32 [4, 64, 64], replicated
- updated_species_mix: float32 [4, 64, 64], replicated
- updated_readout_weights: float32 [2, 64], replicated
- updated_moment_radial_input: float32 [8, 64], replicated
- updated_moment_radial_hidden: float32 [2, 64, 64], replicated
- updated_moment_radial_output: float32 [64, 256], replicated
- updated_moment_degree_mix: float32 [4, 64, 64], replicated
- updated_moment_species_mix: float32 [4, 64, 64], replicated
- updated_moment_readout_weights: float32 [2, 64], replicated
- updated_square_radial_input: float32 [8, 64], replicated
- updated_square_radial_hidden: float32 [2, 64, 64], replicated
- updated_square_radial_output: float32 [64, 256], replicated
- updated_square_degree_mix: float32 [4, 64, 64], replicated
- updated_square_species_mix: float32 [4, 64, 64], replicated
- updated_square_readout_weights: float32 [2, 64], replicated
The draws below stay inside these ranges and needn't reach their ends.
Inputs may be any that keep to these rules, and one draw needn't show every extreme that they name: `edge_source`: indices into the device's extended list: its own 512 atoms, then 128 atoms from the lower and from the upper neighbour along gx, gy, gz in that order. `edge_target`: local atom of the same device. `edge_count`: slots at this position of the device's list or later are unused; some device uses all 2048. `halo_index`: row 2k lists local atoms that the upper neighbour along the k-th axis reads, row 2k + 1 those that the lower one reads; repeats are allowed. `edge_vectors`: every column has a length between 0.8 and 4.95.
All inputs are finite; a program needn't handle non-finite values.
Results may differ from the reference program's by a relative error of at most 0.004.
The reference program's roundings to bfloat16 on the way count: a program that leaves them out, or rounds other values in their place, can miss the bound.
Values may be sent and summed in bfloat16 or wider, within the bound.
No kernel may reach another device: no remote copies, remote signals or barrier semaphores. Data moves between devices by JAX's collectives and lax.ppermute only.
A program may use at most 128 MiB of HBM per device.

```python
import math
import jax
import jax.numpy as jnp
import numpy as np
from jax import lax

C = 64
RADIAL_WIDTH = 64
NBASIS = 8
SPECIES = 4
STEP = 10
A_DEV = 512
E_DEV = 2048
HALO_F = 128
AVG = 2
ATOMS = 16384
EDGES = 65536
HALO_TOT = 4096
N_GX = 2
N_GY = 4
N_GZ = 4
DEVICES = 32


def draw_edge_vectors(key, part):
    key = jax.random.fold_in(key, 11)
    key_length, key_cosine, key_angle = jax.random.split(key, 3)
    length = jax.random.uniform(key_length, (EDGES,), jnp.float32, 1.0, 4.8)
    cosine = jax.random.uniform(key_cosine, (EDGES,), jnp.float32, -1.0, 1.0)
    azimuth = jax.random.uniform(key_angle, (EDGES,), jnp.float32, -math.pi, math.pi)
    sine = jnp.sqrt(jnp.maximum(1.0 - cosine * cosine, 0.0))
    return jnp.stack([length * sine * jnp.cos(azimuth), length * sine * jnp.sin(azimuth), length * cosine])


def with_ends(drawn, key, low, largest):
    spot = [jax.random.randint(jax.random.fold_in(key, axis), (), 0, length) for axis, length in enumerate(drawn.shape)]
    main_axis = drawn.shape.index(max(drawn.shape))
    next_to = spot[:main_axis] + [(spot[main_axis] + 1) % drawn.shape[main_axis]] + spot[main_axis + 1:]
    return drawn.at[tuple(spot)].set(low).at[tuple(next_to)].set(largest)


def block_levels(stream_key, shape, shards, smallest, largest):
    def one(axis_at, blocks):
        heights = jax.random.uniform(jax.random.fold_in(jax.random.fold_in(stream_key, 6), axis_at), (blocks,), jnp.float32, smallest / len(shards), largest / len(shards))
        return jnp.repeat(jnp.exp(heights), shape[axis_at] // blocks).reshape((-1,) + (1,) * (len(shape) - axis_at - 1))

    gain = one(*shards[0])
    for cut in shards[1:]:
        gain = gain * one(*cut)
    return gain


def profile(number_of, total, limit, lean):
    loads = [(1 << 20) // math.isqrt(rank ** lean) + 1 for rank in range(2, number_of + 1)]
    rest, holding = total - limit - (number_of - 1), [1] * (number_of - 1)
    while rest > 0:
        free = [i for i in range(number_of - 1) if holding[i] < limit]
        pool, left = sum([loads[i] for i in free]), rest
        for i in free:
            more = min(limit - holding[i], max(1, left * loads[i] // pool), rest)
            holding[i] = holding[i] + more
            rest = rest - more
    return np.array([limit] + holding)


def ragged_sizes(key, amount, total, most, skew):
    if amount == 2:
        one = jax.random.randint(key, (), max(1, total - most), min(most, total - 1) + 1)
        return jnp.stack([one, total - one])
    tallies = jnp.asarray(profile(amount, total, most, skew), jnp.int32)
    twos = (amount - 1) // 2
    giver, taker = tallies[1:1 + 2 * twos:2], tallies[2:2 + 2 * twos:2]
    margin = jnp.minimum(giver - 1, most - taker)
    moved = jax.random.randint(jax.random.fold_in(key, 1), (twos,), 0, 1 << 20) % (margin + 1)
    tallies = tallies.at[1:1 + 2 * twos:2].set(giver - moved).at[2:2 + 2 * twos:2].set(taker + moved)
    return tallies[jax.random.permutation(jax.random.fold_in(key, 2), amount)]


def bell_draw(own_key, dims, deviation, most, shards=(), kind=jnp.bfloat16):
    entries = jax.random.normal(own_key, dims, jnp.float32) * deviation
    if len(shards) > 0:
        entries = block_levels(own_key, dims, shards, -0.22, 0.18) * entries
    return jnp.clip(entries, min=-most, max=most).astype(kind)


def setup_inputs(seed: int = 0) -> dict:
    streams_of = jax.random.split(jax.random.key(seed), 27)
    node_feats = bell_draw(streams_of[0], (C, ATOMS), 1.0, 6.0, ((1, 32),))
    edge_vectors = draw_edge_vectors(jax.random.fold_in(streams_of[26], 71), 0)
    edge_source = with_ends(jax.random.randint(streams_of[2], (EDGES,), 0, A_DEV + 6 * HALO_F), jax.random.fold_in(streams_of[2], 1), 0, (A_DEV + 6 * HALO_F) - 1).astype(jnp.int32)
    edge_target = with_ends(jax.random.randint(streams_of[3], (EDGES,), 0, A_DEV), jax.random.fold_in(streams_of[3], 1), 0, A_DEV - 1).astype(jnp.int32)
    edge_count = ragged_sizes(streams_of[4], DEVICES, DEVICES * E_DEV * 5 // 8, E_DEV, 2).astype(jnp.int32)
    halo_index = with_ends(jax.random.randint(streams_of[5], (6, HALO_TOT), 0, A_DEV), jax.random.fold_in(streams_of[5], 1), 0, A_DEV - 1).astype(jnp.int32)
    atom_species = with_ends(jax.random.randint(streams_of[6], (ATOMS,), 0, SPECIES), jax.random.fold_in(streams_of[6], 1), 0, SPECIES - 1).astype(jnp.int32)
    site_cotangent = bell_draw(streams_of[7], (ATOMS,), 1.0, 6.0, ((0, 32),), jnp.float32)
    radial_input = bell_draw(streams_of[8], (NBASIS, RADIAL_WIDTH), 2.0, 12.0, (), jnp.float32)
    radial_hidden = bell_draw(streams_of[9], (2, RADIAL_WIDTH, RADIAL_WIDTH), 0.2, 1.2, (), jnp.float32)
    radial_output = bell_draw(streams_of[10], (RADIAL_WIDTH, 4 * C), RADIAL_WIDTH ** -0.5, 0.75, (), jnp.float32)
    degree_mix = bell_draw(streams_of[11], (4, C, C), C ** -0.5, 0.75, (), jnp.float32)
    species_mix = bell_draw(streams_of[12], (SPECIES, C, C), C ** -0.5, 0.75, (), jnp.float32)
    readout_weights = bell_draw(streams_of[13], (2, C), C ** -0.5, 0.75, (), jnp.float32)
    moment_radial_input = bell_draw(streams_of[14], (NBASIS, RADIAL_WIDTH), (0.011 * ATOMS ** 0.5), 6.0, (), jnp.float32)
    moment_radial_hidden = bell_draw(streams_of[15], (2, RADIAL_WIDTH, RADIAL_WIDTH), (0.011 * ATOMS ** 0.5), 6.0, (), jnp.float32)
    moment_radial_output = bell_draw(streams_of[16], (RADIAL_WIDTH, 4 * C), (0.011 * ATOMS ** 0.5), 6.0, (), jnp.float32)
    moment_degree_mix = bell_draw(streams_of[17], (4, C, C), (0.011 * ATOMS ** 0.5), 6.0, (), jnp.float32)
    moment_species_mix = bell_draw(streams_of[18], (SPECIES, C, C), (0.011 * ATOMS ** 0.5), 6.0, (), jnp.float32)
    moment_readout_weights = bell_draw(streams_of[19], (2, C), (0.055 * ATOMS ** 0.5), 40.0, (), jnp.float32)
    square_radial_input = jnp.clip(jnp.exp(jax.random.uniform(streams_of[20], (NBASIS, RADIAL_WIDTH), jnp.float32, math.log(0.16384), math.log(0.65536))), 0.16384, 0.65536)
    square_radial_hidden = jnp.clip(jnp.exp(jax.random.uniform(streams_of[21], (2, RADIAL_WIDTH, RADIAL_WIDTH), jnp.float32, math.log(0.16384), math.log(0.65536))), 0.16384, 0.65536)
    square_radial_output = jnp.clip(jnp.exp(jax.random.uniform(streams_of[22], (RADIAL_WIDTH, 4 * C), jnp.float32, math.log(0.16384), math.log(0.65536))), 0.16384, 0.65536)
    square_degree_mix = jnp.clip(jnp.exp(jax.random.uniform(streams_of[23], (4, C, C), jnp.float32, math.log(0.16384), math.log(0.65536))), 0.16384, 0.65536)
    square_species_mix = jnp.clip(jnp.exp(jax.random.uniform(streams_of[24], (SPECIES, C, C), jnp.float32, math.log(0.16384), math.log(0.65536))), 0.16384, 0.65536)
    square_readout_weights = jnp.clip(jnp.exp(jax.random.uniform(streams_of[25], (2, C), jnp.float32, math.log(4.096), math.log(16.384))), 4.096, 16.384)
    return dict(node_feats=node_feats, edge_vectors=edge_vectors, edge_source=edge_source, edge_target=edge_target, edge_count=edge_count, halo_index=halo_index, atom_species=atom_species, site_cotangent=site_cotangent, radial_input=radial_input, radial_hidden=radial_hidden, radial_output=radial_output, degree_mix=degree_mix, species_mix=species_mix, readout_weights=readout_weights, moment_radial_input=moment_radial_input, moment_radial_hidden=moment_radial_hidden, moment_radial_output=moment_radial_output, moment_degree_mix=moment_degree_mix, moment_species_mix=moment_species_mix, moment_readout_weights=moment_readout_weights, square_radial_input=square_radial_input, square_radial_hidden=square_radial_hidden, square_radial_output=square_radial_output, square_degree_mix=square_degree_mix, square_species_mix=square_species_mix, square_readout_weights=square_readout_weights)


CUTOFF = 5.0
BESSEL_NORM = math.sqrt(2.0 / 5.0)
SQRT3 = math.sqrt(3.0)
SQRT5 = math.sqrt(5.0)
SQRT7 = math.sqrt(7.0)
SQRT15 = math.sqrt(15.0)
CUBIC_A = math.sqrt(35.0 / 8.0)
CUBIC_B = math.sqrt(105.0)
CUBIC_C = math.sqrt(21.0 / 8.0)
BETA_ONE = 0.9
BETA_TWO = 0.999
EPSILON = 1e-08
DECAY = 0.01
RATES = (2.0, 0.2, 0.125, 0.125, 0.125, 0.125)
DEGREE_SLICES = ((0, 1), (1, 4), (4, 9), (9, 16))

@jax.custom_vjp
def low(v):
    return lax.optimization_barrier(v.astype(jnp.bfloat16)).astype(jnp.float32)

@jax.custom_vjp
def low_back(v):
    return v

def low_keep(v):
    return (low(v), None)

def low_pass(kept, grad):
    return (grad,)

def back_keep(v):
    return (v, None)

def back_low(kept, grad):
    return (low(grad),)
low.defvjp(low_keep, low_pass)
low_back.defvjp(back_keep, back_low)

def harmonics(direction):
    along_x, along_y, along_z = (direction[0], direction[1], direction[2])
    square_z = along_z * along_z
    return jnp.stack([jnp.ones_like(along_x), SQRT3 * along_x, SQRT3 * along_y, SQRT3 * along_z, SQRT15 * along_x * along_y, SQRT15 * along_y * along_z, 0.5 * SQRT5 * (3.0 * square_z - 1.0), SQRT15 * along_x * along_z, 0.5 * SQRT15 * (along_x * along_x - along_y * along_y), CUBIC_A * along_y * (3.0 * along_x * along_x - along_y * along_y), CUBIC_B * along_x * along_y * along_z, CUBIC_C * along_y * (5.0 * square_z - 1.0), 0.5 * SQRT7 * along_z * (5.0 * square_z - 3.0), CUBIC_C * along_x * (5.0 * square_z - 1.0), 0.5 * CUBIC_B * along_z * (along_x * along_x - along_y * along_y), CUBIC_A * along_x * (along_x * along_x - 3.0 * along_y * along_y)])

def geometry(relative):
    distance = jnp.sqrt(lax.optimization_barrier(jnp.sum(relative * relative, axis=0)))
    scaled_dist = distance / CUTOFF
    power_six = scaled_dist ** 6
    envelope = 1.0 - 28.0 * power_six + 48.0 * power_six * scaled_dist - 21.0 * power_six * scaled_dist * scaled_dist
    orders = jnp.arange(1, NBASIS + 1).astype(relative.dtype)[:, None]
    bessel = BESSEL_NORM * jnp.sin(orders * (math.pi / CUTOFF) * distance[None, :]) / distance[None, :] * envelope[None, :]
    return (bessel, harmonics(relative / distance[None, :]))

def mixdot(form, left, right):
    return jnp.einsum(form, left, right, precision=lax.Precision.HIGHEST)

def adamw_update(weight, moment, square, gradient, step_rate):
    moment = BETA_ONE * moment + (1.0 - BETA_ONE) * gradient
    square = BETA_TWO * square + (1.0 - BETA_TWO) * gradient * gradient
    corrected = moment / (1.0 - BETA_ONE ** STEP) / (jnp.sqrt(square / (1.0 - BETA_TWO ** STEP)) + EPSILON)
    return (weight - step_rate * (corrected + DECAY * weight), moment, square)

def device_energy(copies, readout, inputs):
    w_in, w_hidden, w_out, w_degree, w_species = copies
    ext_features, ext_displace, vectors, sources, targets, live_mask, species = inputs
    relative = vectors + ext_displace[:, sources] - ext_displace[:, targets]
    bessel, harmonic = geometry(relative)
    pre_one = low_back(mixdot('fk,fe->ke', w_in, low(bessel)))
    act_one = low(jax.nn.silu(pre_one))
    pre_two = low_back(mixdot('fk,fe->ke', w_hidden[0], act_one))
    act_two = low(jax.nn.silu(pre_two))
    pre_three = low_back(mixdot('fk,fe->ke', w_hidden[1], act_two))
    act_three = low(jax.nn.silu(pre_three))
    radial = low_back(mixdot('fk,fe->ke', w_out, act_three)).reshape(4, C, E_DEV)
    weighted = ext_features[:, sources] * live_mask[None, :]
    message = jnp.concatenate([radial[degree][None] * harmonic[first:last, None, :] * weighted[None] for degree, (first, last) in enumerate(DEGREE_SLICES)], axis=0)
    summed = jnp.zeros((16, C, A_DEV), jnp.float32).at[:, :, targets].add(message) * (1.0 / AVG)
    summed_low = low(summed)
    mixed = low_back(jnp.concatenate([mixdot('cd,kci->kdi', w_degree[degree], summed_low[first:last]) for degree, (first, last) in enumerate(DEGREE_SLICES)], axis=0))
    species_mask = (species[None, :] == jnp.arange(SPECIES, dtype=jnp.int32)[:, None]).astype(jnp.float32)
    self_term = low_back(lax.optimization_barrier(jnp.sum(mixdot('zcd,ci->zdi', w_species, ext_features[:, :A_DEV]) * species_mask[:, None, :], axis=0)))
    scalars = mixed[0] + self_term
    gate = jax.nn.sigmoid(scalars)
    gated = mixed[1:] * gate[None]
    quadratic = lax.optimization_barrier(jnp.sum(gated * gated, axis=0))
    return lax.optimization_barrier(jnp.sum(readout[0][:, None] * (scalars * gate) + readout[1][:, None] * quadratic, axis=0))

def reference(node_feats, edge_vectors, edge_source, edge_target, edge_count, halo_index, atom_species, site_cotangent, radial_input, radial_hidden, radial_output, degree_mix, species_mix, readout_weights, moment_radial_input, moment_radial_hidden, moment_radial_output, moment_degree_mix, moment_species_mix, moment_readout_weights, square_radial_input, square_radial_hidden, square_radial_output, square_degree_mix, square_species_mix, square_readout_weights):
    device_total = N_GX * N_GY * N_GZ
    masters = (radial_input, radial_hidden, radial_output, degree_mix, species_mix, readout_weights)
    moments = (moment_radial_input, moment_radial_hidden, moment_radial_output, moment_degree_mix, moment_species_mix, moment_readout_weights)
    squares = (square_radial_input, square_radial_hidden, square_radial_output, square_degree_mix, square_species_mix, square_readout_weights)
    face_index = halo_index.reshape(6, N_GX, N_GY, N_GZ, HALO_F)

    def extend(field):
        row_count = field.shape[0]
        lattice = field.reshape(row_count, N_GX, N_GY, N_GZ, A_DEV)
        pieces = [lattice]
        for axis_pos in range(3):
            upper_list = jnp.broadcast_to(face_index[2 * axis_pos][None], (row_count, N_GX, N_GY, N_GZ, HALO_F))
            lower_list = jnp.broadcast_to(face_index[2 * axis_pos + 1][None], (row_count, N_GX, N_GY, N_GZ, HALO_F))
            upper_face = jnp.take_along_axis(lattice, upper_list, axis=4)
            lower_face = jnp.take_along_axis(lattice, lower_list, axis=4)
            pieces.append(jnp.roll(upper_face, 1, axis=1 + axis_pos))
            pieces.append(jnp.roll(lower_face, -1, axis=1 + axis_pos))
        joined = jnp.concatenate(pieces, axis=4)
        return jnp.transpose(joined.reshape(row_count, device_total, A_DEV + 6 * HALO_F), (1, 0, 2))
    vectors = jnp.transpose(edge_vectors.reshape(3, device_total, E_DEV), (1, 0, 2))
    sources = edge_source.reshape(device_total, E_DEV)
    targets = edge_target.reshape(device_total, E_DEV)
    species = atom_species.reshape(device_total, A_DEV)
    live_mask = (jnp.arange(E_DEV, dtype=jnp.int32)[None, :] < edge_count[:, None]).astype(jnp.float32)

    def energies(features, displacement, w_in, w_hidden, w_out, w_degree, w_species, readout):
        copies = (low(w_in), low(w_hidden), low(w_out), low(w_degree), low(w_species))
        ext_features = extend(features)
        ext_displace = extend(displacement)
        per_device = lax.map(lambda inputs: jax.checkpoint(device_energy)(copies, readout, inputs), (ext_features, ext_displace, vectors, sources, targets, live_mask, species))
        return per_device.reshape(ATOMS)
    features = node_feats.astype(jnp.float32)
    displacement = jnp.zeros((3, ATOMS), jnp.float32)
    site_energy, pullback = jax.vjp(energies, features, displacement, *masters)
    grads = pullback(site_cotangent)
    updated = [adamw_update(masters[member], moments[member], squares[member], grads[2 + member], RATES[member]) for member in range(6)]
    return (site_energy, grads[0], grads[1], updated[0][0], updated[1][0], updated[2][0], updated[3][0], updated[4][0], updated[5][0], updated[0][1], updated[1][1], updated[2][1], updated[3][1], updated[4][1], updated[5][1], updated[0][2], updated[1][2], updated[2][2], updated[3][2], updated[4][2], updated[5][2])
```

```python
import math

import jax
import jax.numpy as jnp
from jax import lax
from jax.experimental import pallas as pl
from jax.experimental.pallas import tpu as pltpu
from jax.sharding import PartitionSpec as P

NBASIS = 8
STEP = 10
CUTOFF = 5.0
BESSEL_NORM = math.sqrt(2.0 / 5.0)
SQRT3 = math.sqrt(3.0)
SQRT5 = math.sqrt(5.0)
SQRT7 = math.sqrt(7.0)
SQRT15 = math.sqrt(15.0)
CUBIC_A = math.sqrt(35.0 / 8.0)
CUBIC_B = math.sqrt(105.0)
CUBIC_C = math.sqrt(21.0 / 8.0)
BETA_ONE = 0.9
BETA_TWO = 0.999
EPSILON = 1e-08
DECAY = 0.01
RATES = (2.0, 0.2, 0.125, 0.125, 0.125, 0.125)
DEGREE_SLICES = ((0, 1), (1, 4), (4, 9), (9, 16))
DEGREE_OF = tuple(d for d, (a, b) in enumerate(DEGREE_SLICES) for _ in range(a, b))
AXES = ("gx", "gy", "gz")
F32 = jnp.float32
BF16 = jnp.bfloat16
LANES = 128
TILE = 256
BACK_ROWS = 80
PACK_ROWS = 456
VMEM_LIMIT = 50 * 1024 * 1024


def dot_nn(left, right):
    return lax.dot_general(left, right, (((1,), (0,)), ((), ())), preferred_element_type=F32)


def dot_nt(left, right):
    return lax.dot_general(left, right, (((1,), (1,)), ((), ())), preferred_element_type=F32)


def dot_tn(left, right):
    return lax.dot_general(left, right, (((0,), (0,)), ((), ())), preferred_element_type=F32)


def halves(values):
    high = values.astype(BF16)
    return high, (values - high.astype(F32)).astype(BF16)


def one_hot(row, count, base=0):
    place = lax.broadcasted_iota(jnp.int32, (count, row.shape[1]), 0) + base
    return jnp.where(place == row, 1.0, 0.0).astype(BF16)


def index_row(rows, first, width):
    start = first // LANES
    return jnp.concatenate(
        [rows[start + n : start + n + 1, :] for n in range(width // LANES)], axis=1
    )


def live_sources(source_ref, count_ref):
    rows = source_ref[...]
    slot = lax.broadcasted_iota(jnp.int32, rows.shape, 0) * LANES + lax.broadcasted_iota(
        jnp.int32, rows.shape, 1
    )
    return jnp.where(slot < count_ref[0], rows, -1)


def column_of(row):
    size = row.shape[1]
    eye = lax.broadcasted_iota(jnp.int32, (size, size), 0) == lax.broadcasted_iota(
        jnp.int32, (size, size), 1
    )
    return jnp.sum(jnp.where(eye, row, 0.0), axis=1, keepdims=True)


def row_of(column):
    size = column.shape[0]
    eye = lax.broadcasted_iota(jnp.int32, (size, size), 0) == lax.broadcasted_iota(
        jnp.int32, (size, size), 1
    )
    return jnp.sum(jnp.where(eye, column, 0.0), axis=0, keepdims=True)


def pick_faces_kernel(feats_ref, halo_ref, *face_refs):
    channels, atoms = feats_ref.shape
    feats = feats_ref[...]
    halo = halo_ref[...]
    face = 0
    for ref in face_refs:
        for part in range(ref.shape[0] // channels):
            picked = dot_nn(feats, one_hot(halo[face : face + 1, :], atoms))
            ref[part * channels : (part + 1) * channels, :] = picked.astype(BF16)
            face += 1


def radial_kernel(
    count_ref,
    feats_ref,
    vectors_ref,
    source_ref,
    species_ref,
    w_in_ref,
    w_hidden_ref,
    w_out_ref,
    w_species_ref,
    own_ref,
    harm_ref,
    geo_ref,
    slope_b_ref,
    bessel_ref,
    act_ref,
    slope_ref,
    radial_ref,
    self_ref,
):
    channels, atoms = feats_ref.shape
    slots = vectors_ref.shape[1]
    vectors = vectors_ref[...]
    vx, vy, vz = vectors[0:1, :], vectors[1:2, :], vectors[2:3, :]
    dist = jnp.sqrt(vx * vx + vy * vy + vz * vz)
    inverse = 1.0 / dist
    x, y, z = vx / dist, vy / dist, vz / dist
    scaled = dist / CUTOFF
    square = scaled * scaled
    five = square * square * scaled
    six = square * square * square
    envelope = 1.0 - 28.0 * six + 48.0 * six * scaled - 21.0 * six * scaled * scaled
    slope_env = (-168.0 * five + 336.0 * six - 168.0 * six * scaled) / CUTOFF
    freq = (lax.broadcasted_iota(jnp.int32, (NBASIS, 1), 0) + 1).astype(F32) * (math.pi / CUTOFF)
    angle = freq * dist
    sine, cosine = jnp.sin(angle), jnp.cos(angle)
    bessel = BESSEL_NORM * sine / dist * envelope
    slope_b_ref[...] = (
        BESSEL_NORM
        * inverse
        * ((freq * cosine - sine * inverse) * envelope + sine * slope_env)
    )
    zz = z * z
    harm_ref[...] = jnp.concatenate(
        [
            jnp.ones_like(x),
            SQRT3 * x,
            SQRT3 * y,
            SQRT3 * z,
            SQRT15 * x * y,
            SQRT15 * y * z,
            0.5 * SQRT5 * (3.0 * zz - 1.0),
            SQRT15 * x * z,
            0.5 * SQRT15 * (x * x - y * y),
            CUBIC_A * y * (3.0 * x * x - y * y),
            CUBIC_B * x * y * z,
            CUBIC_C * y * (5.0 * zz - 1.0),
            0.5 * SQRT7 * z * (5.0 * zz - 3.0),
            CUBIC_C * x * (5.0 * zz - 1.0),
            0.5 * CUBIC_B * z * (x * x - y * y),
            CUBIC_A * x * (x * x - 3.0 * y * y),
        ],
        axis=0,
    )
    geo_ref[0:3, :] = jnp.concatenate([x, y, z], axis=0)
    geo_ref[3:4, :] = inverse
    w_in = w_in_ref[...].astype(BF16)
    low = bessel.astype(BF16)
    bessel_ref[...] = low
    weights = [w_in, w_hidden_ref[0].astype(BF16), w_hidden_ref[1].astype(BF16)]
    for layer, weight in enumerate(weights):
        pre = dot_tn(weight, low)
        logistic = jax.nn.sigmoid(pre)
        low = (pre * logistic).astype(BF16)
        act_ref[layer] = low
        slope_ref[layer] = logistic * (1.0 + pre * (1.0 - logistic))
    radial_ref[...] = dot_tn(w_out_ref[...].astype(BF16), low)

    feats = feats_ref[...]
    kinds = w_species_ref.shape[0]
    species = species_ref[...]
    species_row = jnp.concatenate(
        [species[n : n + 1, :] for n in range(species.shape[0])], axis=1
    )
    total = jnp.zeros((channels, atoms), F32)
    for kind in range(kinds):
        masked = jnp.where(species_row == kind, feats.astype(F32), 0.0).astype(BF16)
        total += dot_tn(w_species_ref[kind].astype(BF16), masked)
    self_ref[...] = total

    sources = live_sources(source_ref, count_ref)
    for first in range(0, slots, TILE):
        hot = one_hot(index_row(sources, first, TILE), atoms)
        own_ref[:, first : first + TILE] = dot_nn(feats, hot).astype(BF16)


def layer_kernel(
    scale,
    face_count,
    count_ref,
    *refs,
):
    face_in = refs[:face_count]
    (
        own_ref,
        harm_ref,
        geo_ref,
        slope_b_ref,
        bessel_ref,
        act_ref,
        slope_ref,
        radial_ref,
        self_ref,
        feats_ref,
        source_ref,
        target_ref,
        species_ref,
        cotangent_ref,
        w_in_ref,
        w_hidden_ref,
        w_out_ref,
        w_degree_ref,
        w_species_ref,
        readout_ref,
    ) = refs[face_count : face_count + 20]
    energy_ref, owned_ref, pack_ref = refs[face_count + 20 : face_count + 23]
    face_out = refs[face_count + 23 : 2 * face_count + 23]
    (
        weighted_ref,
        message_ref,
        summed_ref,
        low_ref,
        mixed_back_ref,
        mixed_radial_ref,
        part_ref,
        harm_back_ref,
        radial_back_ref,
        stack_ref,
        target_hot_ref,
        source_hot_ref,
    ) = refs[2 * face_count + 23 :]
    channels, atoms = feats_ref.shape
    slots = harm_ref.shape[1]
    kinds = w_species_ref.shape[0]
    extended = source_hot_ref.shape[0]
    harm_count = harm_ref.shape[0]
    w_degree = [w_degree_ref[d].astype(BF16) for d in range(4)]

    sources = live_sources(source_ref, count_ref)
    targets = target_ref[...]
    pieces = []
    for ref in face_in:
        for part in range(ref.shape[0] // channels):
            pieces.append(ref[part * channels : (part + 1) * channels, :])
    borrowed = jnp.concatenate(pieces, axis=1)
    for first in range(0, slots, TILE):
        cols = slice(first, first + TILE)
        hot = one_hot(index_row(sources, first, TILE), extended)
        source_hot_ref[:, cols] = hot
        target_hot_ref[:, cols] = one_hot(index_row(targets, first, TILE), atoms)
        weighted_ref[:, cols] = (
            own_ref[:, cols].astype(F32) + dot_nn(borrowed, hot[atoms:, :])
        ) * scale

    for first in range(0, slots, TILE):
        cols = slice(first, first + TILE)
        weighted = weighted_ref[:, cols]
        scaled = [radial_ref[d * channels : (d + 1) * channels, cols] * weighted for d in range(4)]
        for k in range(harm_count):
            high, rest = halves(scaled[DEGREE_OF[k]] * harm_ref[k : k + 1, cols])
            message_ref[k * channels : (k + 1) * channels, :TILE] = high
            message_ref[k * channels : (k + 1) * channels, TILE:] = rest
        hot = target_hot_ref[:, cols]
        added = dot_nt(message_ref[...], jnp.concatenate([hot, hot], axis=1))
        if first == 0:
            summed_ref[...] = added
        else:
            summed_ref[...] += added

    total_square = jnp.zeros((channels, atoms), F32)
    scalars = self_ref[...]
    for k in range(harm_count):
        rows = slice(k * channels, (k + 1) * channels)
        low = summed_ref[rows, :].astype(BF16)
        low_ref[rows, :] = low
        mixed = dot_tn(w_degree[DEGREE_OF[k]], low)
        if k == 0:
            scalars = scalars + mixed
        else:
            summed_ref[rows, :] = mixed
            total_square += mixed * mixed
    cotangent = cotangent_ref[...]
    cotangent = jnp.concatenate(
        [cotangent[n : n + 1, :] for n in range(cotangent.shape[0])], axis=1
    )
    readout_scalar = column_of(readout_ref[0:1, :])
    readout_square = column_of(readout_ref[1:2, :])
    gate = jax.nn.sigmoid(scalars)
    scalar_out = scalars * gate
    quadratic = total_square * (gate * gate)
    energy_ref[...] = jnp.sum(
        readout_scalar * scalar_out + readout_square * quadratic, axis=0, keepdims=True
    )
    grad_readout = jnp.concatenate(
        [
            row_of(jnp.sum(scalar_out * cotangent, axis=1, keepdims=True)),
            row_of(jnp.sum(quadratic * cotangent, axis=1, keepdims=True)),
            jnp.zeros((6, channels), F32),
        ],
        axis=0,
    )
    back_quad = 2.0 * (readout_square * cotangent) * gate
    back_scalars = (readout_scalar * cotangent) * (
        gate * (1.0 + scalars * (1.0 - gate))
    ) + back_quad * total_square * (gate * (1.0 - gate))
    back_self = back_scalars.astype(BF16)
    mixed_back_ref[0:channels, :] = back_self
    factor = back_quad * gate
    for k in range(1, harm_count):
        rows = slice(k * channels, (k + 1) * channels)
        mixed_back_ref[rows, :] = (summed_ref[rows, :] * factor).astype(BF16)
    grad_degree = []
    for first, last in DEGREE_SLICES:
        total = jnp.zeros((channels, channels), F32)
        for k in range(first, last):
            rows = slice(k * channels, (k + 1) * channels)
            total += dot_nt(low_ref[rows, :], mixed_back_ref[rows, :])
        grad_degree.append(total)
    species = species_ref[...]
    species_row = jnp.concatenate(
        [species[n : n + 1, :] for n in range(species.shape[0])], axis=1
    )
    feats = feats_ref[...].astype(F32)
    back_local = jnp.zeros((channels, atoms), F32)
    grad_species = []
    for kind in range(kinds):
        mask = species_row == kind
        grad_species.append(dot_nt(jnp.where(mask, feats, 0.0).astype(BF16), back_self))
        back_local += dot_nn(
            w_species_ref[kind].astype(BF16), jnp.where(mask, back_scalars, 0.0).astype(BF16)
        )

    for d in range(4):
        rows = slice(d * channels, (d + 1) * channels)
        high, rest = halves(radial_ref[rows, :] * weighted_ref[...])
        mixed_radial_ref[rows, :] = dot_tn(w_degree[d], high) + dot_tn(w_degree[d], rest)
    for first in range(0, slots, TILE):
        cols = slice(first, first + TILE)
        gathered = dot_nn(mixed_back_ref[...], target_hot_ref[:, cols])
        for d, (begin, end) in enumerate(DEGREE_SLICES):
            part = jnp.zeros((channels, TILE), F32)
            mixed_radial = mixed_radial_ref[d * channels : (d + 1) * channels, cols]
            for k in range(begin, end):
                piece = gathered[k * channels : (k + 1) * channels, :]
                part += piece * harm_ref[k : k + 1, cols]
                harm_back_ref[k : k + 1, cols] = jnp.sum(
                    piece * mixed_radial, axis=0, keepdims=True
                )
            part_ref[d * channels : (d + 1) * channels, cols] = part
    back_weighted = jnp.zeros((channels, slots), F32)
    for d in range(4):
        rows = slice(d * channels, (d + 1) * channels)
        high, rest = halves(part_ref[rows, :])
        mixed_part = dot_nn(w_degree[d], high) + dot_nn(w_degree[d], rest)
        radial_back_ref[rows, :] = (mixed_part * weighted_ref[...]).astype(BF16)
        back_weighted += mixed_part * radial_ref[rows, :]
    back_weighted = back_weighted * scale
    high, rest = halves(back_weighted)
    stack_ref[0:channels, :] = high
    stack_ref[BACK_ROWS : BACK_ROWS + channels, :] = rest

    radial_back = radial_back_ref[...]
    grad_out = dot_nt(act_ref[2], radial_back)
    back_pre = (dot_nn(w_out_ref[...].astype(BF16), radial_back) * slope_ref[2]).astype(BF16)
    grad_hidden_two = dot_nt(act_ref[1], back_pre)
    back_pre = (dot_nn(w_hidden_ref[1].astype(BF16), back_pre) * slope_ref[1]).astype(BF16)
    grad_hidden_one = dot_nt(act_ref[0], back_pre)
    back_pre = (dot_nn(w_hidden_ref[0].astype(BF16), back_pre) * slope_ref[0]).astype(BF16)
    grad_in = dot_nt(bessel_ref[...], back_pre)
    back_bessel = dot_nn(w_in_ref[...].astype(BF16), back_pre)

    back_dist = jnp.sum(back_bessel * slope_b_ref[...], axis=0, keepdims=True)
    x, y, z, inverse = (geo_ref[n : n + 1, :] for n in range(4))
    g = [None] + [harm_back_ref[k : k + 1, :] for k in range(1, harm_count)]
    xx, yy, zz = x * x, y * y, z * z
    five = CUBIC_C * (5.0 * zz - 1.0)
    three = 3.0 * CUBIC_A * (xx - yy)
    cross = 6.0 * CUBIC_A * x * y
    along_x = (
        SQRT3 * g[1]
        + SQRT15 * (y * g[4] + z * g[7] + x * g[8])
        + cross * g[9]
        + CUBIC_B * (y * z * g[10] + z * x * g[14])
        + five * g[13]
        + three * g[15]
    )
    along_y = (
        SQRT3 * g[2]
        + SQRT15 * (x * g[4] + z * g[5] - y * g[8])
        + three * g[9]
        + CUBIC_B * (x * z * g[10] - z * y * g[14])
        + five * g[11]
        - cross * g[15]
    )
    along_z = (
        SQRT3 * g[3]
        + SQRT15 * (y * g[5] + x * g[7])
        + 3.0 * SQRT5 * z * g[6]
        + CUBIC_B * (x * y * g[10] + 0.5 * (xx - yy) * g[14])
        + 10.0 * CUBIC_C * z * (y * g[11] + x * g[13])
        + 1.5 * SQRT7 * (5.0 * zz - 1.0) * g[12]
    )
    inward = back_dist - inverse * (x * along_x + y * along_y + z * along_z)
    back_relative = jnp.concatenate(
        [
            inverse * along_x + x * inward,
            inverse * along_y + y * inward,
            inverse * along_z + z * inward,
            jnp.zeros((BACK_ROWS - channels - 3, slots), F32),
        ],
        axis=0,
    )
    high, rest = halves(back_relative)
    stack_ref[channels:BACK_ROWS, :] = high
    stack_ref[BACK_ROWS + channels :, :] = rest
    spread = dot_nt(stack_ref[...], source_hot_ref[...])
    spread = spread[:BACK_ROWS, :] + spread[BACK_ROWS:, :]
    target_back = dot_nt(jnp.concatenate([high, rest], axis=0), target_hot_ref[...])
    size = BACK_ROWS - channels
    target_back = target_back[:size, :] + target_back[size:, :]
    owned_ref[0:channels, :] = spread[:channels, :atoms] + back_local
    owned_ref[channels:, :] = spread[channels:, :atoms] - target_back
    face = 0
    for ref in face_out:
        for part in range(ref.shape[0] // BACK_ROWS):
            start = atoms + face * LANES
            ref[part * BACK_ROWS : (part + 1) * BACK_ROWS, :] = spread[:, start : start + LANES]
            face += 1

    pack_ref[0:64, :] = grad_out[:, :LANES]
    pack_ref[64:128, :] = grad_out[:, LANES:]
    pack_ref[128:192, :] = jnp.concatenate([grad_degree[0], grad_degree[1]], axis=1)
    pack_ref[192:256, :] = jnp.concatenate([grad_degree[2], grad_degree[3]], axis=1)
    pack_ref[256:320, :] = jnp.concatenate([grad_species[0], grad_species[1]], axis=1)
    pack_ref[320:384, :] = jnp.concatenate([grad_species[2], grad_species[3]], axis=1)
    pack_ref[384:448, :] = jnp.concatenate([grad_hidden_one, grad_hidden_two], axis=1)
    pack_ref[448:456, :] = jnp.concatenate([grad_in, grad_readout], axis=1)
    if pack_ref.shape[0] > PACK_ROWS:
        pack_ref[PACK_ROWS:, :] = jnp.zeros((pack_ref.shape[0] - PACK_ROWS, LANES), F32)


def collect_kernel(face_count, parts_ref, owned_ref, halo_ref, *refs):
    face_in = refs[:face_count]
    share_ref, feature_ref, position_ref = refs[face_count:]
    channels, atoms = feature_ref.shape
    devices = parts_ref.shape[0]
    total = parts_ref[0].astype(F32)
    for n in range(1, devices):
        total += parts_ref[n].astype(F32)
    for n in range(devices):
        share_ref[n] = total
    pieces = []
    for ref in face_in:
        for part in range(ref.shape[0] // BACK_ROWS):
            pieces.append(ref[part * BACK_ROWS : (part + 1) * BACK_ROWS, :])
    returned = jnp.concatenate(pieces, axis=1)
    high, rest = halves(returned)
    halo = halo_ref[...]
    hot = jnp.concatenate(
        [one_hot(halo[face : face + 1, :], atoms) for face in range(halo.shape[0])], axis=1
    )
    added = dot_nt(jnp.concatenate([high, rest], axis=0), hot)
    owned = owned_ref[...] + added[:BACK_ROWS, :] + added[BACK_ROWS:, :]
    feature_ref[...] = owned[:channels, :]
    position_ref[...] = owned[channels : channels + 3, :]


def update_kernel(grad_ref, *refs):
    masters, moments, squares = refs[0:6], refs[6:12], refs[12:18]
    outs = refs[18:]

    def step(member, index, gradient):
        weight = masters[member][index]
        moment = BETA_ONE * moments[member][index] + (1.0 - BETA_ONE) * gradient
        square = BETA_TWO * squares[member][index] + (1.0 - BETA_TWO) * gradient * gradient
        corrected = (
            moment
            / (1.0 - BETA_ONE**STEP)
            / (jnp.sqrt(square / (1.0 - BETA_TWO**STEP)) + EPSILON)
        )
        outs[member][index] = weight - RATES[member] * (corrected + DECAY * weight)
        outs[6 + member][index] = moment
        outs[12 + member][index] = square

    step(0, Ellipsis, grad_ref[448:456, :64])
    step(1, 0, grad_ref[384:448, :64])
    step(1, 1, grad_ref[384:448, 64:])
    step(2, (slice(None), slice(0, LANES)), grad_ref[0:64, :])
    step(2, (slice(None), slice(LANES, 2 * LANES)), grad_ref[64:128, :])
    for base, member in ((128, 3), (256, 4)):
        for n in range(4):
            first = base + 64 * (n // 2)
            half = 64 * (n % 2)
            step(member, n, grad_ref[first : first + 64, half : half + 64])
    step(5, Ellipsis, grad_ref[448:450, 64:])


def shifted(value, axis, steps):
    count = lax.axis_size(axis)
    pairs = [(source, (source + steps) % count) for source in range(count)]
    return lax.ppermute(value, axis, pairs)


def vmem(count):
    return [pl.BlockSpec(memory_space=pltpu.VMEM)] * count


def shape(dims, dtype=F32):
    return jax.ShapeDtypeStruct(dims, dtype)


def on_device(*arguments):
    (
        node_feats,
        edge_vectors,
        edge_source,
        edge_target,
        edge_count,
        halo_index,
        atom_species,
        site_cotangent,
    ) = arguments[:8]
    masters, moments, squares = arguments[8:14], arguments[14:20], arguments[20:26]
    radial_input, radial_hidden, radial_output, degree_mix, species_mix, readout_weights = masters
    channels, atoms = node_feats.shape
    slots = edge_vectors.shape[1]
    width = halo_index.shape[1]
    extended = atoms + 6 * width
    devices = lax.axis_size(AXES)
    scale = 1.0 / max(1, 5 * slots // (8 * atoms))
    share = -(-PACK_ROWS // devices)
    share = -(-share // 8) * 8
    params = pltpu.CompilerParams(vmem_limit_bytes=VMEM_LIMIT)
    smem = [pl.BlockSpec(memory_space=pltpu.SMEM)]

    routes = []
    for axis in AXES:
        if lax.axis_size(axis) == 2:
            routes.append((axis, 1, 2))
        else:
            routes.append((axis, 1, 1))
            routes.append((axis, -1, 1))

    source = edge_source.reshape(slots // LANES, LANES)
    target = edge_target.reshape(slots // LANES, LANES)
    species = atom_species.reshape(atoms // LANES, LANES)
    cotangent = site_cotangent.reshape(atoms // LANES, LANES)

    faces = pl.pallas_call(
        pick_faces_kernel,
        out_shape=[shape((parts * channels, width), BF16) for _, _, parts in routes],
        in_specs=vmem(2),
        out_specs=vmem(len(routes)),
        compiler_params=params,
        name="pick_faces",
    )(node_feats, halo_index)
    arrived = [shifted(face, axis, way) for face, (axis, way, _) in zip(faces, routes)]

    edge_parts = pl.pallas_call(
        radial_kernel,
        out_shape=[
            shape((channels, slots), BF16),
            shape((16, slots)),
            shape((4, slots)),
            shape((NBASIS, slots)),
            shape((NBASIS, slots), BF16),
            shape((3, channels, slots), BF16),
            shape((3, channels, slots)),
            shape((4 * channels, slots)),
            shape((channels, atoms)),
        ],
        in_specs=smem + vmem(8),
        out_specs=vmem(9),
        compiler_params=params,
        name="radial",
        cost_estimate=pl.CostEstimate(
            flops=2 * slots * 64 * 1024, bytes_accessed=8 << 20, transcendentals=0
        ),
    )(
        edge_count,
        node_feats,
        edge_vectors,
        source,
        species,
        radial_input,
        radial_hidden,
        radial_output,
        species_mix,
    )

    results = pl.pallas_call(
        lambda *refs: layer_kernel(scale, len(routes), *refs),
        out_shape=[
            shape((1, atoms)),
            shape((BACK_ROWS, atoms)),
            shape((share * devices, LANES)),
        ]
        + [shape((parts * BACK_ROWS, width)) for _, _, parts in routes],
        in_specs=smem + vmem(len(routes) + 20),
        out_specs=vmem(3 + len(routes)),
        scratch_shapes=[
            pltpu.VMEM((channels, slots), F32),
            pltpu.VMEM((16 * channels, 2 * TILE), BF16),
            pltpu.VMEM((16 * channels, atoms), F32),
            pltpu.VMEM((16 * channels, atoms), BF16),
            pltpu.VMEM((16 * channels, atoms), BF16),
            pltpu.VMEM((4 * channels, slots), F32),
            pltpu.VMEM((4 * channels, slots), F32),
            pltpu.VMEM((16, slots), F32),
            pltpu.VMEM((4 * channels, slots), BF16),
            pltpu.VMEM((2 * BACK_ROWS, slots), BF16),
            pltpu.VMEM((atoms, slots), BF16),
            pltpu.VMEM((extended, slots), BF16),
        ],
        compiler_params=params,
        name="layer",
    )(
        edge_count,
        *arrived,
        *edge_parts,
        node_feats,
        source,
        target,
        species,
        cotangent,
        radial_input,
        radial_hidden,
        radial_output,
        degree_mix,
        species_mix,
        readout_weights,
    )
    energy, owned, packed = results[:3]
    returned = [
        shifted(back, axis, -way) for back, (axis, way, _) in zip(results[3:], routes)
    ]
    parts = lax.all_to_all(packed.reshape(devices, share, LANES), AXES, 0, 0, tiled=True)
    shares, feature_grad, position_grad = pl.pallas_call(
        lambda *refs: collect_kernel(len(routes), *refs),
        out_shape=[
            shape((devices, share, LANES)),
            shape((channels, atoms)),
            shape((3, atoms)),
        ],
        in_specs=vmem(3 + len(routes)),
        out_specs=vmem(3),
        compiler_params=params,
        name="collect",
    )(parts, owned, halo_index, *returned)
    gradient = lax.all_to_all(shares, AXES, 0, 0, tiled=True).reshape(devices * share, LANES)
    updated = pl.pallas_call(
        update_kernel,
        out_shape=[shape(member.shape) for member in masters + masters + masters],
        in_specs=vmem(19),
        out_specs=vmem(18),
        compiler_params=params,
        name="update",
    )(gradient, *masters, *moments, *squares)
    return (energy.reshape(atoms), feature_grad, position_grad, *updated)


def solution(mesh):
    split = P(AXES)
    split_last = P(None, AXES)
    in_specs = (
        split_last,
        split_last,
        split,
        split,
        split,
        split_last,
        split,
        split,
    ) + (P(),) * 18
    out_specs = (split, split_last, split_last) + (P(),) * 18
    return jax.shard_map(
        on_device, mesh=mesh, in_specs=in_specs, out_specs=out_specs, check_vma=False
    )
```

```python
import math

import jax
import jax.numpy as jnp
from jax import lax
from jax.experimental import pallas as pl
from jax.experimental.pallas import tpu as pltpu
from jax.sharding import PartitionSpec as P

NBASIS = 8
STEP = 10
CUTOFF = 5.0
BESSEL_NORM = math.sqrt(2.0 / 5.0)
SQRT3 = math.sqrt(3.0)
SQRT5 = math.sqrt(5.0)
SQRT7 = math.sqrt(7.0)
SQRT15 = math.sqrt(15.0)
CUBIC_A = math.sqrt(35.0 / 8.0)
CUBIC_B = math.sqrt(105.0)
CUBIC_C = math.sqrt(21.0 / 8.0)
BETA_ONE = 0.9
BETA_TWO = 0.999
EPSILON = 1e-08
DECAY = 0.01
RATES = (2.0, 0.2, 0.125, 0.125, 0.125, 0.125)
DEGREE_SLICES = ((0, 1), (1, 4), (4, 9), (9, 16))
DEGREE_OF = tuple(d for d, (a, b) in enumerate(DEGREE_SLICES) for _ in range(a, b))
AXES = ("gx", "gy", "gz")
F32 = jnp.float32
BF16 = jnp.bfloat16
LANES = 128
TILE = 256
BACK_ROWS = 80
PACK_ROWS = 456
VMEM_LIMIT = 24 * 1024 * 1024


def dot_nn(left, right):
    return lax.dot_general(left, right, (((1,), (0,)), ((), ())), preferred_element_type=F32)


def dot_nt(left, right):
    return lax.dot_general(left, right, (((1,), (1,)), ((), ())), preferred_element_type=F32)


def dot_tn(left, right):
    return lax.dot_general(left, right, (((0,), (0,)), ((), ())), preferred_element_type=F32)


def halves(values):
    high = values.astype(BF16)
    return high, (values - high.astype(F32)).astype(BF16)


def one_hot(row, count, base=0):
    place = lax.broadcasted_iota(jnp.int32, (count, row.shape[1]), 0) + base
    return jnp.where(place == row, 1.0, 0.0).astype(BF16)


def index_row(rows, first, width):
    start = first // LANES
    return jnp.concatenate(
        [rows[start + n : start + n + 1, :] for n in range(width // LANES)], axis=1
    )


def live_sources(source_ref, count_ref):
    rows = source_ref[...]
    slot = lax.broadcasted_iota(jnp.int32, rows.shape, 0) * LANES + lax.broadcasted_iota(
        jnp.int32, rows.shape, 1
    )
    return jnp.where(slot < count_ref[0], rows, -1)


def column_of(row):
    size = row.shape[1]
    eye = lax.broadcasted_iota(jnp.int32, (size, size), 0) == lax.broadcasted_iota(
        jnp.int32, (size, size), 1
    )
    return jnp.sum(jnp.where(eye, row, 0.0), axis=1, keepdims=True)


def row_of(column):
    size = column.shape[0]
    eye = lax.broadcasted_iota(jnp.int32, (size, size), 0) == lax.broadcasted_iota(
        jnp.int32, (size, size), 1
    )
    return jnp.sum(jnp.where(eye, column, 0.0), axis=0, keepdims=True)


def fetch(pairs, sems):
    copies = [
        pltpu.make_async_copy(source, place, sems.at[n]) for n, (source, place) in enumerate(pairs)
    ]
    for copy in copies:
        copy.start()
    return copies


def pick_faces_kernel(feats_in, halo_in, feats_ref, *refs):
    face_refs, (halo_ref, sems) = refs[:-2], refs[-2:]
    channels, atoms = feats_ref.shape
    for copy in fetch([(feats_in, feats_ref), (halo_in, halo_ref)], sems):
        copy.wait()
    feats = feats_ref[...]
    halo = halo_ref[...]
    face = 0
    for ref in face_refs:
        for part in range(ref.shape[0] // channels):
            picked = dot_nn(feats, one_hot(halo[face : face + 1, :], atoms))
            ref[part * channels : (part + 1) * channels, :] = picked.astype(BF16)
            face += 1


def radial_kernel(
    count_ref,
    feats_ref,
    vectors_in,
    source_in,
    target_in,
    species_in,
    cotangent_in,
    w_in_in,
    w_hidden_in,
    w_out_in,
    w_degree_in,
    w_species_in,
    readout_in,
    own_ref,
    harm_ref,
    geo_ref,
    slope_b_ref,
    bessel_ref,
    act_ref,
    slope_ref,
    radial_ref,
    self_ref,
    source_ref,
    target_ref,
    species_ref,
    cotangent_ref,
    readout_ref,
    w_in_ref,
    w_hidden_ref,
    w_out_ref,
    w_degree_ref,
    w_species_ref,
    vectors_ref,
    w_in_full,
    w_hidden_full,
    w_out_full,
    w_degree_full,
    w_species_full,
    sems,
):
    copies = fetch(
        [
            (vectors_in, vectors_ref),
            (w_in_in, w_in_full),
            (w_hidden_in, w_hidden_full),
            (w_out_in, w_out_full),
            (w_species_in, w_species_full),
            (species_in, species_ref),
            (source_in, source_ref),
            (w_degree_in, w_degree_full),
            (target_in, target_ref),
            (cotangent_in, cotangent_ref),
            (readout_in, readout_ref),
        ],
        sems,
    )
    copies[0].wait()
    channels, atoms = feats_ref.shape
    slots = vectors_ref.shape[1]
    vectors = vectors_ref[...]
    vx, vy, vz = vectors[0:1, :], vectors[1:2, :], vectors[2:3, :]
    dist = jnp.sqrt(vx * vx + vy * vy + vz * vz)
    inverse = 1.0 / dist
    x, y, z = vx / dist, vy / dist, vz / dist
    scaled = dist / CUTOFF
    square = scaled * scaled
    five = square * square * scaled
    six = square * square * square
    envelope = 1.0 - 28.0 * six + 48.0 * six * scaled - 21.0 * six * scaled * scaled
    slope_env = (-168.0 * five + 336.0 * six - 168.0 * six * scaled) / CUTOFF
    freq = (lax.broadcasted_iota(jnp.int32, (NBASIS, 1), 0) + 1).astype(F32) * (math.pi / CUTOFF)
    angle = freq * dist
    sine, cosine = jnp.sin(angle), jnp.cos(angle)
    bessel = BESSEL_NORM * sine / dist * envelope
    slope_b_ref[...] = (
        BESSEL_NORM
        * inverse
        * ((freq * cosine - sine * inverse) * envelope + sine * slope_env)
    )
    zz = z * z
    harm_ref[...] = jnp.concatenate(
        [
            jnp.ones_like(x),
            SQRT3 * x,
            SQRT3 * y,
            SQRT3 * z,
            SQRT15 * x * y,
            SQRT15 * y * z,
            0.5 * SQRT5 * (3.0 * zz - 1.0),
            SQRT15 * x * z,
            0.5 * SQRT15 * (x * x - y * y),
            CUBIC_A * y * (3.0 * x * x - y * y),
            CUBIC_B * x * y * z,
            CUBIC_C * y * (5.0 * zz - 1.0),
            0.5 * SQRT7 * z * (5.0 * zz - 3.0),
            CUBIC_C * x * (5.0 * zz - 1.0),
            0.5 * CUBIC_B * z * (x * x - y * y),
            CUBIC_A * x * (x * x - 3.0 * y * y),
        ],
        axis=0,
    )
    geo_ref[0:3, :] = jnp.concatenate([x, y, z], axis=0)
    geo_ref[3:4, :] = inverse
    for copy in copies[1:]:
        copy.wait()
    w_in_ref[...] = w_in_full[...].astype(BF16)
    w_hidden_ref[...] = w_hidden_full[...].astype(BF16)
    w_out_ref[...] = w_out_full[...].astype(BF16)
    w_degree_ref[...] = w_degree_full[...].astype(BF16)
    w_species_ref[...] = w_species_full[...].astype(BF16)
    low = bessel.astype(BF16)
    bessel_ref[...] = low
    weights = [w_in_ref[...], w_hidden_ref[0], w_hidden_ref[1]]
    for layer, weight in enumerate(weights):
        pre = dot_tn(weight, low)
        logistic = jax.nn.sigmoid(pre)
        low = (pre * logistic).astype(BF16)
        act_ref[layer] = low
        slope_ref[layer] = logistic * (1.0 + pre * (1.0 - logistic))
    radial_ref[...] = dot_tn(w_out_ref[...], low)

    feats = feats_ref[...]
    kinds = w_species_ref.shape[0]
    species = species_ref[...]
    species_row = jnp.concatenate(
        [species[n : n + 1, :] for n in range(species.shape[0])], axis=1
    )
    total = jnp.zeros((channels, atoms), F32)
    for kind in range(kinds):
        masked = jnp.where(species_row == kind, feats.astype(F32), 0.0).astype(BF16)
        total += dot_tn(w_species_ref[kind], masked)
    self_ref[...] = total

    sources = live_sources(source_ref, count_ref)
    source_ref[...] = sources
    for first in range(0, slots, TILE):
        hot = one_hot(index_row(sources, first, TILE), atoms)
        own_ref[:, first : first + TILE] = dot_nn(feats, hot).astype(BF16)


def layer_kernel(scale, face_count, *refs):
    face_in = refs[:face_count]
    (
        own_ref,
        harm_ref,
        geo_ref,
        slope_b_ref,
        bessel_ref,
        act_ref,
        slope_ref,
        radial_ref,
        self_ref,
        feats_ref,
        source_ref,
        target_ref,
        species_ref,
        cotangent_ref,
        readout_ref,
        w_in_ref,
        w_hidden_ref,
        w_out_ref,
        w_degree_ref,
        w_species_ref,
        energy_ref,
        pack_ref,
        edge_back_ref,
        back_local_ref,
        target_hot_ref,
        weighted_ref,
        message_ref,
        summed_ref,
        low_ref,
        mixed_back_ref,
        mixed_radial_ref,
        part_ref,
        radial_back_ref,
    ) = refs[face_count:]
    channels, atoms = feats_ref.shape
    slots = harm_ref.shape[1]
    kinds = w_species_ref.shape[0]
    borrow_count = 6 * LANES
    harm_count = harm_ref.shape[0]
    w_degree = [w_degree_ref[d] for d in range(4)]

    sources = source_ref[...]
    targets = target_ref[...]
    pieces = []
    for ref in face_in:
        for part in range(ref.shape[0] // channels):
            pieces.append(ref[part * channels : (part + 1) * channels, :])
    borrowed = jnp.concatenate(pieces, axis=1)
    for first in range(0, slots, TILE):
        cols = slice(first, first + TILE)
        hot = one_hot(index_row(sources, first, TILE), borrow_count, atoms)
        target_hot_ref[:, cols] = one_hot(index_row(targets, first, TILE), atoms)
        weighted_ref[:, cols] = (
            own_ref[:, cols].astype(F32) + dot_nn(borrowed, hot)
        ) * scale

    for first in range(0, slots, TILE):
        cols = slice(first, first + TILE)
        weighted = weighted_ref[:, cols]
        scaled = [radial_ref[d * channels : (d + 1) * channels, cols] * weighted for d in range(4)]
        for k in range(harm_count):
            high, rest = halves(scaled[DEGREE_OF[k]] * harm_ref[k : k + 1, cols])
            message_ref[k * channels : (k + 1) * channels, :TILE] = high
            message_ref[k * channels : (k + 1) * channels, TILE:] = rest
        hot = target_hot_ref[:, cols]
        added = dot_nt(message_ref[...], jnp.concatenate([hot, hot], axis=1))
        if first == 0:
            summed_ref[...] = added
        else:
            summed_ref[...] += added

    total_square = jnp.zeros((channels, atoms), F32)
    scalars = self_ref[...]
    for k in range(harm_count):
        rows = slice(k * channels, (k + 1) * channels)
        low = summed_ref[rows, :].astype(BF16)
        low_ref[rows, :] = low
        mixed = dot_tn(w_degree[DEGREE_OF[k]], low)
        if k == 0:
            scalars = scalars + mixed
        else:
            summed_ref[rows, :] = mixed
            total_square += mixed * mixed
    cotangent = cotangent_ref[...]
    cotangent = jnp.concatenate(
        [cotangent[n : n + 1, :] for n in range(cotangent.shape[0])], axis=1
    )
    readout_scalar = column_of(readout_ref[0:1, :])
    readout_square = column_of(readout_ref[1:2, :])
    gate = jax.nn.sigmoid(scalars)
    scalar_out = scalars * gate
    quadratic = total_square * (gate * gate)
    energy_ref[...] = jnp.sum(
        readout_scalar * scalar_out + readout_square * quadratic, axis=0, keepdims=True
    )
    grad_readout = jnp.concatenate(
        [
            row_of(jnp.sum(scalar_out * cotangent, axis=1, keepdims=True)),
            row_of(jnp.sum(quadratic * cotangent, axis=1, keepdims=True)),
            jnp.zeros((6, channels), F32),
        ],
        axis=0,
    )
    back_quad = 2.0 * (readout_square * cotangent) * gate
    back_scalars = (readout_scalar * cotangent) * (
        gate * (1.0 + scalars * (1.0 - gate))
    ) + back_quad * total_square * (gate * (1.0 - gate))
    back_self = back_scalars.astype(BF16)
    mixed_back_ref[0:channels, :] = back_self
    factor = back_quad * gate
    for k in range(1, harm_count):
        rows = slice(k * channels, (k + 1) * channels)
        mixed_back_ref[rows, :] = (summed_ref[rows, :] * factor).astype(BF16)
    grad_degree = []
    for first, last in DEGREE_SLICES:
        total = jnp.zeros((channels, channels), F32)
        for k in range(first, last):
            rows = slice(k * channels, (k + 1) * channels)
            total += dot_nt(low_ref[rows, :], mixed_back_ref[rows, :])
        grad_degree.append(total)
    species = species_ref[...]
    species_row = jnp.concatenate(
        [species[n : n + 1, :] for n in range(species.shape[0])], axis=1
    )
    feats = feats_ref[...].astype(F32)
    back_local = jnp.zeros((channels, atoms), F32)
    grad_species = []
    for kind in range(kinds):
        mask = species_row == kind
        grad_species.append(dot_nt(jnp.where(mask, feats, 0.0).astype(BF16), back_self))
        back_local += dot_nn(
            w_species_ref[kind], jnp.where(mask, back_scalars, 0.0).astype(BF16)
        )
    back_local_ref[...] = back_local

    for d in range(4):
        rows = slice(d * channels, (d + 1) * channels)
        high, rest = halves(radial_ref[rows, :] * weighted_ref[...])
        mixed_radial_ref[rows, :] = dot_tn(w_degree[d], high) + dot_tn(w_degree[d], rest)
    for first in range(0, slots, TILE):
        cols = slice(first, first + TILE)
        gathered = dot_nn(mixed_back_ref[...], target_hot_ref[:, cols])
        for d, (begin, end) in enumerate(DEGREE_SLICES):
            part = jnp.zeros((channels, TILE), F32)
            mixed_radial = mixed_radial_ref[d * channels : (d + 1) * channels, cols]
            for k in range(begin, end):
                piece = gathered[k * channels : (k + 1) * channels, :]
                part += piece * harm_ref[k : k + 1, cols]
                edge_back_ref[channels + k : channels + k + 1, cols] = jnp.sum(
                    piece * mixed_radial, axis=0, keepdims=True
                )
            part_ref[d * channels : (d + 1) * channels, cols] = part
    back_weighted = jnp.zeros((channels, slots), F32)
    for d in range(4):
        rows = slice(d * channels, (d + 1) * channels)
        high, rest = halves(part_ref[rows, :])
        mixed_part = dot_nn(w_degree[d], high) + dot_nn(w_degree[d], rest)
        radial_back_ref[rows, :] = (mixed_part * weighted_ref[...]).astype(BF16)
        back_weighted += mixed_part * radial_ref[rows, :]
    edge_back_ref[0:channels, :] = back_weighted * scale

    radial_back = radial_back_ref[...]
    grad_out = dot_nt(act_ref[2], radial_back)
    back_pre = (dot_nn(w_out_ref[...], radial_back) * slope_ref[2]).astype(BF16)
    grad_hidden_two = dot_nt(act_ref[1], back_pre)
    back_pre = (dot_nn(w_hidden_ref[1], back_pre) * slope_ref[1]).astype(BF16)
    grad_hidden_one = dot_nt(act_ref[0], back_pre)
    back_pre = (dot_nn(w_hidden_ref[0], back_pre) * slope_ref[0]).astype(BF16)
    grad_in = dot_nt(bessel_ref[...], back_pre)
    back_bessel = dot_nn(w_in_ref[...], back_pre)
    edge_back_ref[channels : channels + 1, :] = jnp.sum(
        back_bessel * slope_b_ref[...], axis=0, keepdims=True
    )
    edge_back_ref[channels + harm_count : channels + harm_count + 4, :] = geo_ref[...]

    def packed(pair):
        return jnp.concatenate(pair, axis=1).astype(pack_ref.dtype)

    pack_ref[0:64, :] = grad_out[:, :LANES].astype(pack_ref.dtype)
    pack_ref[64:128, :] = grad_out[:, LANES:].astype(pack_ref.dtype)
    pack_ref[128:192, :] = packed([grad_degree[0], grad_degree[1]])
    pack_ref[192:256, :] = packed([grad_degree[2], grad_degree[3]])
    pack_ref[256:320, :] = packed([grad_species[0], grad_species[1]])
    pack_ref[320:384, :] = packed([grad_species[2], grad_species[3]])
    pack_ref[384:448, :] = packed([grad_hidden_one, grad_hidden_two])
    pack_ref[448:456, :] = packed([grad_in, grad_readout])
    if pack_ref.shape[0] > PACK_ROWS:
        pack_ref[PACK_ROWS:, :] = jnp.zeros((pack_ref.shape[0] - PACK_ROWS, LANES), pack_ref.dtype)


def spread_kernel(
    count_ref,
    edge_back_in,
    back_local_in,
    source_in,
    target_in,
    owned_ref,
    *refs,
):
    face_out, refs = refs[:-6], refs[-6:]
    edge_back_ref, back_local_ref, source_ref, target_ref, stack_ref, sems = refs
    copies = fetch(
        [
            (source_in, source_ref),
            (target_in, target_ref),
            (edge_back_in, edge_back_ref),
            (back_local_in, back_local_ref),
        ],
        sems,
    )
    channels, atoms = back_local_ref.shape
    slots = edge_back_ref.shape[1]
    harm_count = 16
    for copy in copies:
        copy.wait()
    sources = live_sources(source_ref, count_ref)
    targets = target_ref[...]
    high, rest = halves(edge_back_ref[0:channels, :])
    stack_ref[0:channels, :] = high
    stack_ref[BACK_ROWS : BACK_ROWS + channels, :] = rest
    back_dist = edge_back_ref[channels : channels + 1, :]
    x, y, z, inverse = (
        edge_back_ref[channels + harm_count + n : channels + harm_count + n + 1, :]
        for n in range(4)
    )
    g = [edge_back_ref[channels + k : channels + k + 1, :] for k in range(harm_count)]
    xx, yy, zz = x * x, y * y, z * z
    five = CUBIC_C * (5.0 * zz - 1.0)
    three = 3.0 * CUBIC_A * (xx - yy)
    cross = 6.0 * CUBIC_A * x * y
    along_x = (
        SQRT3 * g[1]
        + SQRT15 * (y * g[4] + z * g[7] + x * g[8])
        + cross * g[9]
        + CUBIC_B * (y * z * g[10] + z * x * g[14])
        + five * g[13]
        + three * g[15]
    )
    along_y = (
        SQRT3 * g[2]
        + SQRT15 * (x * g[4] + z * g[5] - y * g[8])
        + three * g[9]
        + CUBIC_B * (x * z * g[10] - z * y * g[14])
        + five * g[11]
        - cross * g[15]
    )
    along_z = (
        SQRT3 * g[3]
        + SQRT15 * (y * g[5] + x * g[7])
        + 3.0 * SQRT5 * z * g[6]
        + CUBIC_B * (x * y * g[10] + 0.5 * (xx - yy) * g[14])
        + 10.0 * CUBIC_C * z * (y * g[11] + x * g[13])
        + 1.5 * SQRT7 * (5.0 * zz - 1.0) * g[12]
    )
    inward = back_dist - inverse * (x * along_x + y * along_y + z * along_z)
    back_relative = jnp.concatenate(
        [
            inverse * along_x + x * inward,
            inverse * along_y + y * inward,
            inverse * along_z + z * inward,
            jnp.zeros((BACK_ROWS - channels - 3, slots), F32),
        ],
        axis=0,
    )
    high, rest = halves(back_relative)
    stack_ref[channels:BACK_ROWS, :] = high
    stack_ref[BACK_ROWS + channels :, :] = rest
    both = jnp.concatenate([high, rest], axis=0)
    spread, target_back = 0.0, 0.0
    for first in range(0, slots, TILE):
        cols = slice(first, first + TILE)
        hot = one_hot(index_row(sources, first, TILE), atoms + 6 * LANES)
        spread += dot_nt(stack_ref[:, cols], hot)
        hot = one_hot(index_row(targets, first, TILE), atoms)
        target_back += dot_nt(both[:, cols], hot)
    spread = spread[:BACK_ROWS, :] + spread[BACK_ROWS:, :]
    size = BACK_ROWS - channels
    target_back = target_back[:size, :] + target_back[size:, :]
    owned_ref[0:channels, :] = spread[:channels, :atoms] + back_local_ref[...]
    owned_ref[channels:, :] = spread[channels:, :atoms] - target_back
    face = 0
    for ref in face_out:
        for part in range(ref.shape[0] // BACK_ROWS):
            start = atoms + face * LANES
            ref[part * BACK_ROWS : (part + 1) * BACK_ROWS, :] = spread[:, start : start + LANES]
            face += 1


def total_kernel(parts_ref, after_ref, share_ref):
    devices = parts_ref.shape[0]
    total = parts_ref[0].astype(F32)
    for n in range(1, devices):
        total += parts_ref[n].astype(F32)
    for n in range(devices):
        share_ref[n] = total


def collect_kernel(owned_in, halo_in, *refs):
    state_in, face_in, state_out = refs[:18], refs[18:-23], refs[-21:-3]
    feature_ref, position_ref = refs[-23:-21]
    owned_ref, halo_ref, sems = refs[-3:]
    pairs = [(halo_in, halo_ref), (owned_in, owned_ref)] + list(zip(state_in, state_out))
    for copy in fetch(pairs, sems):
        copy.wait()
    channels, atoms = feature_ref.shape
    pieces = []
    for ref in face_in:
        for part in range(ref.shape[0] // BACK_ROWS):
            pieces.append(ref[part * BACK_ROWS : (part + 1) * BACK_ROWS, :])
    returned = jnp.concatenate(pieces, axis=1)
    high, rest = halves(returned)
    halo = halo_ref[...]
    hot = jnp.concatenate(
        [one_hot(halo[face : face + 1, :], atoms) for face in range(halo.shape[0])], axis=1
    )
    added = dot_nt(jnp.concatenate([high, rest], axis=0), hot)
    owned = owned_ref[...] + added[:BACK_ROWS, :] + added[BACK_ROWS:, :]
    feature_ref[...] = owned[:channels, :]
    position_ref[...] = owned[channels : channels + 3, :]


def update_kernel(grad_ref, *refs):
    masters, moments, squares = refs[0:6], refs[6:12], refs[12:18]
    outs = refs[18:]

    def step(member, index, gradient):
        weight = masters[member][index]
        moment = BETA_ONE * moments[member][index] + (1.0 - BETA_ONE) * gradient
        square = BETA_TWO * squares[member][index] + (1.0 - BETA_TWO) * gradient * gradient
        corrected = (
            moment
            / (1.0 - BETA_ONE**STEP)
            / (jnp.sqrt(square / (1.0 - BETA_TWO**STEP)) + EPSILON)
        )
        outs[member][index] = weight - RATES[member] * (corrected + DECAY * weight)
        outs[6 + member][index] = moment
        outs[12 + member][index] = square

    step(0, Ellipsis, grad_ref[448:456, :64])
    step(1, 0, grad_ref[384:448, :64])
    step(1, 1, grad_ref[384:448, 64:])
    step(2, (slice(None), slice(0, LANES)), grad_ref[0:64, :])
    step(2, (slice(None), slice(LANES, 2 * LANES)), grad_ref[64:128, :])
    for base, member in ((128, 3), (256, 4)):
        for n in range(4):
            first = base + 64 * (n // 2)
            half = 64 * (n % 2)
            step(member, n, grad_ref[first : first + 64, half : half + 64])
    step(5, Ellipsis, grad_ref[448:450, 64:])


def shifted(value, axis, steps):
    count = lax.axis_size(axis)
    pairs = [(source, (source + steps) % count) for source in range(count)]
    return lax.ppermute(value, axis, pairs)


def in_hbm(arrays):
    return [pltpu.with_memory_space_constraint(array, pltpu.HBM) for array in arrays]


def vmem(count):
    return [pl.BlockSpec(memory_space=pltpu.VMEM)] * count


def shape(dims, dtype=F32):
    return jax.ShapeDtypeStruct(dims, dtype)


def on_device(*arguments):
    (
        node_feats,
        edge_vectors,
        edge_source,
        edge_target,
        edge_count,
        halo_index,
        atom_species,
        site_cotangent,
    ) = arguments[:8]
    masters, moments, squares = arguments[8:14], arguments[14:20], arguments[20:26]
    radial_input, radial_hidden, radial_output, degree_mix, species_mix, readout_weights = masters
    channels, atoms = node_feats.shape
    slots = edge_vectors.shape[1]
    width = halo_index.shape[1]
    devices = lax.axis_size(AXES)
    scale = 1.0 / max(1, 5 * slots // (8 * atoms))
    share = -(-PACK_ROWS // devices)
    share = -(-share // 8) * 8
    params = pltpu.CompilerParams(vmem_limit_bytes=VMEM_LIMIT)
    smem = [pl.BlockSpec(memory_space=pltpu.SMEM)]
    hbm = pl.BlockSpec(memory_space=pltpu.HBM)

    routes = []
    for axis in AXES:
        if lax.axis_size(axis) == 2:
            routes.append((axis, 1, 2))
        else:
            routes.append((axis, 1, 1))
            routes.append((axis, -1, 1))

    source = edge_source.reshape(slots // LANES, LANES)
    target = edge_target.reshape(slots // LANES, LANES)
    species = atom_species.reshape(atoms // LANES, LANES)
    cotangent = site_cotangent.reshape(atoms // LANES, LANES)

    feats, *faces = pl.pallas_call(
        pick_faces_kernel,
        out_shape=[shape((channels, atoms), BF16)]
        + [shape((parts * channels, width), BF16) for _, _, parts in routes],
        in_specs=[hbm] * 2,
        out_specs=vmem(1 + len(routes)),
        scratch_shapes=[
            pltpu.VMEM(halo_index.shape, jnp.int32),
            pltpu.SemaphoreType.DMA((2,)),
        ],
        compiler_params=params,
        name="pick_faces",
    )(*in_hbm((node_feats, halo_index)))
    arrived = [shifted(face, axis, way) for face, (axis, way, _) in zip(faces, routes)]

    sized = (radial_input, radial_hidden, radial_output, degree_mix, species_mix)
    own, harm, geo, slope_b, *rest = pl.pallas_call(
        radial_kernel,
        out_shape=[
            shape((channels, slots), BF16),
            shape((16, slots)),
            shape((4, slots)),
            shape((NBASIS, slots)),
            shape((NBASIS, slots), BF16),
            shape((3, channels, slots), BF16),
            shape((3, channels, slots)),
            shape((4 * channels, slots)),
            shape((channels, atoms)),
            shape(source.shape, jnp.int32),
            shape(target.shape, jnp.int32),
            shape(species.shape, jnp.int32),
            shape(cotangent.shape),
            shape(readout_weights.shape),
        ]
        + [shape(member.shape, BF16) for member in sized],
        in_specs=smem + vmem(1) + [hbm] * 11,
        out_specs=vmem(19),
        scratch_shapes=[pltpu.VMEM(edge_vectors.shape, F32)]
        + [pltpu.VMEM(member.shape, F32) for member in sized]
        + [pltpu.SemaphoreType.DMA((11,))],
        compiler_params=params,
        name="radial",
        cost_estimate=pl.CostEstimate(
            flops=2 * slots * 64 * 1024, bytes_accessed=8 << 20, transcendentals=0
        ),
    )(
        edge_count,
        feats,
        *in_hbm(
            (edge_vectors, source, target, species, cotangent) + sized + (readout_weights,)
        ),
    )

    state = masters + moments + squares
    energy, packed, edge_back, back_local = pl.pallas_call(
        lambda *refs: layer_kernel(scale, len(routes), *refs),
        out_shape=[
            shape((1, atoms)),
            shape((share * devices, LANES)),
            pltpu.HBM((channels + 24, slots), F32),
            pltpu.HBM((channels, atoms), F32),
        ],
        in_specs=vmem(len(routes) + 20),
        out_specs=vmem(4),
        scratch_shapes=[
            pltpu.VMEM((atoms, slots), BF16),
            pltpu.VMEM((channels, slots), F32),
            pltpu.VMEM((16 * channels, 2 * TILE), BF16),
            pltpu.VMEM((16 * channels, atoms), F32),
            pltpu.VMEM((16 * channels, atoms), BF16),
            pltpu.VMEM((16 * channels, atoms), BF16),
            pltpu.VMEM((4 * channels, slots), F32),
            pltpu.VMEM((4 * channels, slots), F32),
            pltpu.VMEM((4 * channels, slots), BF16),
        ],
        compiler_params=params,
        name="layer",
    )(*arrived, own, harm, geo, slope_b, *rest[:5], feats, *rest[5:])
    parts = lax.all_to_all(packed.reshape(devices, share, LANES), AXES, 0, 0, tiled=True)
    owned, *returns = pl.pallas_call(
        spread_kernel,
        out_shape=[pltpu.HBM((BACK_ROWS, atoms), F32)]
        + [pltpu.HBM((parts * BACK_ROWS, width), F32) for _, _, parts in routes],
        in_specs=smem + [hbm] * 4,
        out_specs=vmem(1 + len(routes)),
        scratch_shapes=[
            pltpu.VMEM((channels + 24, slots), F32),
            pltpu.VMEM((channels, atoms), F32),
            pltpu.VMEM(source.shape, jnp.int32),
            pltpu.VMEM(target.shape, jnp.int32),
            pltpu.VMEM((2 * BACK_ROWS, slots), BF16),
            pltpu.SemaphoreType.DMA((4,)),
        ],
        compiler_params=params,
        name="spread",
        cost_estimate=pl.CostEstimate(
            flops=2 * slots * 160 * 2048, bytes_accessed=8 << 20, transcendentals=0
        ),
    )(edge_count, *in_hbm((edge_back, back_local, source, target)))
    returned = [shifted(back, axis, -way) for back, (axis, way, _) in zip(returns, routes)]
    shares = pl.pallas_call(
        total_kernel,
        out_shape=shape((devices, share, LANES)),
        in_specs=vmem(1) + [hbm],
        out_specs=vmem(1)[0],
        compiler_params=params,
        name="total",
        cost_estimate=pl.CostEstimate(
            flops=1 << 33, bytes_accessed=8 << 20, transcendentals=0
        ),
    )(parts, *in_hbm((owned,)))
    gradient = lax.all_to_all(shares, AXES, 0, 0, tiled=True).reshape(devices * share, LANES)
    feature_grad, position_grad, *state = pl.pallas_call(
        collect_kernel,
        out_shape=[shape((channels, atoms)), shape((3, atoms))]
        + [shape(member.shape) for member in state],
        in_specs=[hbm] * 20 + vmem(len(routes)),
        out_specs=vmem(20),
        scratch_shapes=[
            pltpu.VMEM((BACK_ROWS, atoms), F32),
            pltpu.VMEM(halo_index.shape, jnp.int32),
            pltpu.SemaphoreType.DMA((20,)),
        ],
        compiler_params=params,
        name="collect",
        cost_estimate=pl.CostEstimate(
            flops=1 << 36, bytes_accessed=1 << 20, transcendentals=0
        ),
    )(*in_hbm((owned, halo_index) + state), *returned)
    updated = pl.pallas_call(
        update_kernel,
        out_shape=[shape(member.shape) for member in masters + masters + masters],
        in_specs=vmem(19),
        out_specs=vmem(18),
        compiler_params=params,
        name="update",
    )(gradient, *state)
    return (energy.reshape(atoms), feature_grad, position_grad, *updated)


def solution(mesh):
    split = P(AXES)
    split_last = P(None, AXES)
    in_specs = (
        split_last,
        split_last,
        split,
        split,
        split,
        split_last,
        split,
        split,
    ) + (P(),) * 18
    out_specs = (split, split_last, split_last) + (P(),) * 18
    return jax.shard_map(
        on_device, mesh=mesh, in_specs=in_specs, out_specs=out_specs, check_vma=False
    )
```
